256 devices in a mesh: cfg: 2 (over core), blk: 16 (over z, x_lo), uly: 8 (over x_hi, y).
Axes of the slice: x: 4 (x_hi: 2, x_lo: 2; x = x_hi * 2 + x_lo), y: 4, z: 8, core: 2. Of those that a mesh axis runs over, the one named last changes fastest.
Arguments:
- queries: bfloat16 [2, 8192, 5120], P('cfg', ('blk', 'uly')), may hold values from -6 to 6
- keys: bfloat16 [2, 8192, 5120], P('cfg', ('blk', 'uly')), may hold values from -6 to 6
- values: bfloat16 [2, 8192, 5120], P('cfg', ('blk', 'uly')), may hold values from -6 to 6
- latent: float32 [8192, 5120], P(('blk', 'uly'), 'cfg'), may hold values from -6 to 6
- previous_velocity: float32 [8192, 5120], P(('blk', 'uly'), 'cfg'), may hold values from -12 to 12
Outputs:
- velocity: float32 [8192, 5120], P(('blk', 'uly'), 'cfg')
- latent_next: float32 [8192, 5120], P(('blk', 'uly'), 'cfg')
The draws below stay inside these ranges and needn't reach their ends.
All inputs are finite; a program needn't handle non-finite values.
Results may differ from the reference program's by a relative error of at most 0.006.
Values may be sent and summed in bfloat16 or wider, within the bound.
A program may use at most 64 MiB of HBM per device.

```python
import math
import jax
import jax.numpy as jnp
from jax import lax

HEADS = 40
HEAD_DIM = 128
D = 5120
TOKENS = 8192


def draw_queries(key, part):
    key = jax.random.fold_in(key, 11)
    result = 1.6 * jax.random.truncated_normal(key, -3.75, 3.75, (2, TOKENS, D), jnp.float32)
    return result.astype(jnp.bfloat16)


def draw_keys(key, part):
    key = jax.random.fold_in(key, 23)
    result = 1.6 * jax.random.truncated_normal(key, -3.75, 3.75, (2, TOKENS, D), jnp.float32)
    return result.astype(jnp.bfloat16)


def levels(own_key, shape, pieces, low, top_value):
    gain = 1.0
    for position, blocks in pieces:
        draws = jax.random.uniform(jax.random.fold_in(jax.random.fold_in(own_key, 6), position), (blocks,), jnp.float32, low / len(pieces), top_value / len(pieces))
        gain = gain * jnp.repeat(jnp.exp(draws), shape[position] // blocks).reshape((-1,) + (1,) * (len(shape) - 1 - position))
    return gain


def gaussian(own_key, shape, scale, bound, pieces=(), kind=jnp.bfloat16):
    level = levels(own_key, shape, pieces, -0.22, 0.18) if pieces else 1.0
    values = jax.random.normal(own_key, shape, jnp.float32) * scale * level
    return jnp.minimum(jnp.maximum(values, -bound), bound).astype(kind)


def setup_inputs(seed: int = 0) -> dict:
    streams_of = jax.random.split(jax.random.key(seed), 6)
    queries = draw_queries(jax.random.fold_in(streams_of[5], 71), 0)
    keys = draw_keys(jax.random.fold_in(streams_of[5], 71), 0)
    values = gaussian(streams_of[2], (2, TOKENS, D), 1.0, 6.0, ((0, 2), (1, 128)))
    latent = gaussian(streams_of[3], (TOKENS, D), 1.0, 6.0, ((0, 128), (1, 2)), jnp.float32)
    previous_velocity = gaussian(streams_of[4], (TOKENS, D), 2.0, 12.0, ((0, 128), (1, 2)), jnp.float32)
    return {"queries": queries, "keys": keys, "values": values, "latent": latent, "previous_velocity": previous_velocity}


guidance_scale = 5.0
step_size = 0.25

def attend(query_rows, key_rows, value_rows):
    length = query_rows.shape[0]

    def by_head(matrix):
        return matrix.reshape(length, HEADS, HEAD_DIM).transpose(1, 0, 2)

    def one_head(block):
        query_head, key_head, value_head = block
        scores = jnp.dot(query_head, key_head.T, preferred_element_type=jnp.float32) * (1.0 / math.sqrt(HEAD_DIM))
        weights = jnp.exp(scores - lax.optimization_barrier(jnp.max(scores, axis=1, keepdims=True)))
        totals = lax.optimization_barrier(jnp.sum(weights, axis=1, keepdims=True))
        weighted = jnp.dot(weights.astype(jnp.bfloat16), value_head, preferred_element_type=jnp.float32)
        return (weighted / totals).astype(jnp.bfloat16)
    outputs = lax.map(one_head, (by_head(query_rows), by_head(key_rows), by_head(value_rows)))
    return outputs.transpose(1, 0, 2).reshape(length, HEADS * HEAD_DIM)

def reference(queries, keys, values, latent, previous_velocity):
    conditional = attend(queries[0], keys[0], values[0]).astype(jnp.float32)
    unconditional = attend(queries[1], keys[1], values[1]).astype(jnp.float32)
    velocity = unconditional + guidance_scale * (conditional - unconditional)
    latent_next = latent + step_size * (1.5 * velocity - 0.5 * previous_velocity)
    return (velocity, latent_next)
```

```python
import functools
import math

import jax
import jax.numpy as jnp
from jax import lax
from jax.experimental import pallas as pl
from jax.experimental.pallas import tpu as pltpu
from jax.sharding import PartitionSpec as P

HEAD_DIM = 128

guidance_scale = 5.0
step_size = 0.25

EXP2_SCALE = math.log2(math.e) / math.sqrt(HEAD_DIM)
MESH = pl.DeviceIdType.MESH
LOOKAHEAD = 1


def nt(left, right):
    return lax.dot_general(
        left, right, (((1,), (1,)), ((), ())), preferred_element_type=jnp.float32
    )


def kernel(
    nz, side, rows,
    q_ref, k_ref, v_ref, out_ref,
    kv, qm, q5, vt, vt5, acc, top, acc5, top5,
    o_send, p_send, l_send, o_got, p_got, l_got, merged,
    q_sem, q5_sem, q5f_sem, kv_sem, fwd_sem, o_sem, p_sem, l_sem, out_sem,
    q_sent, kv_sent, q5f_sent, fwd_sent, o_sent, p_sent, l_sent, out_sent,
):
    heads = side + 1
    half = nz // 2
    group = half * rows
    block = nz * rows
    queries = side * block
    c = lax.axis_index("cfg")
    blk = lax.axis_index("blk")
    uly = lax.axis_index("uly")
    z = lax.div(blk, 2)
    x = lax.div(uly, side) * 2 + lax.rem(blk, 2)
    y = lax.rem(uly, side)
    a = x * (1 - c) + y * c
    b = y * (1 - c) + x * c

    def chip(x_, y_, z_, core):
        return (core, z_ * 2 + lax.rem(x_, 2), lax.div(x_, 2) * side + y_)

    def dev(a_, b_, z_, core=None):
        return chip(a_ * (1 - c) + b_ * c, b_ * (1 - c) + a_ * c, z_, c if core is None else core)

    def minus(value, steps, count):
        return lax.rem(value + count - steps, count)

    def plus(value, steps, count):
        return lax.rem(value + steps, count)

    def remote(src, dst, sent, got, device):
        return pltpu.make_async_remote_copy(
            src_ref=src, dst_ref=dst, send_sem=sent, recv_sem=got,
            device_id=device, device_id_type=MESH,
        )

    def await_bytes(ref, sem):
        pltpu.make_async_copy(ref, ref, sem).wait()

    barrier = pltpu.get_barrier_semaphore()

    def greet(device):
        pl.semaphore_signal(barrier, inc=1, device_id=device, device_id_type=MESH)

    def greet_layer(s, _):
        z_ = minus(z, s, nz)
        for r in range(side):
            greet(dev(minus(a, r, side), b, z_))
        greet(chip(x, y, z_, 1 - c))
        return 0

    for r in range(1, side):
        greet(dev(minus(a, r, side), b, z))
        greet(dev(a, minus(b, r, side), z))
        greet(chip(minus(x, r, side), y, z, 1 - c))
        greet(chip(x, minus(y, r, side), z, 1 - c))
    greet(chip(x, y, z, 1 - c))
    lax.fori_loop(1, nz, greet_layer, 0)
    pl.semaphore_wait(barrier, 4 * (side - 1) + 1 + (nz - 1) * (side + 1))

    def cols(z_, head):
        return pl.ds(pl.multiple_of((z_ * heads + head) * HEAD_DIM, HEAD_DIM), HEAD_DIM)

    def order(i):
        back = lax.rem(nz - lax.div(i, 2), nz)
        odd = lax.rem(i, 2)
        return odd * lax.div(i + 1, 2) + (1 - odd) * back

    def send_q(s, z_, first):
        for r in range(first, side):
            a_ = minus(a, r, side)
            remote(q_ref.at[0, :, cols(z_, a_)], qm.at[r, s], q_sent.at[s], q_sem,
                   dev(a_, b, z_)).start()

    def send_kv(s, z_, first):
        for r in range(first, side):
            a_ = minus(a, r, side)
            for part, ref in ((0, k_ref), (1, v_ref)):
                remote(ref.at[0, :, cols(z_, a_)], kv.at[s, part, 0, r], kv_sent.at[s],
                       kv_sem.at[s], dev(a_, b, z_)).start()

    def send_q_layer(i, _):
        s = order(i)
        z_ = minus(z, s, nz)
        remote(q_ref.at[0, :, cols(z_, side)], q5.at[0, s], q_sent.at[s], q5_sem,
               dev(a, b, z_)).start()
        send_q(s, z_, 0)
        return 0

    def send_kv_layer(i, _):
        s = order(i)
        z_ = minus(z, s, nz)
        send_kv(s, z_, 0)
        for part, ref in ((0, k_ref), (1, v_ref)):
            remote(ref.at[0, :, cols(z_, side)], kv.at[s, part, 0, side], kv_sent.at[s],
                   kv_sem.at[s], dev(a, b, z_)).start()
        return 0

    pltpu.make_async_copy(q_ref.at[0, :, cols(z, side)], q5.at[0, 0], q5_sem).start()
    pltpu.make_async_copy(q_ref.at[0, :, cols(z, a)], qm.at[0, 0], q_sem).start()
    for part, ref in ((0, k_ref), (1, v_ref)):
        pltpu.make_async_copy(ref.at[0, :, cols(z, a)], kv.at[0, part, 0, 0], kv_sem.at[0]).start()
        pltpu.make_async_copy(ref.at[0, :, cols(z, side)], kv.at[0, part, 0, side], kv_sem.at[0]).start()
    lax.fori_loop(1, nz, send_q_layer, 0)
    send_q(0, z, 1)
    send_kv(0, z, 1)
    lax.fori_loop(1, nz, send_kv_layer, 0)

    acc[...] = jnp.zeros_like(acc)
    top[...] = jnp.full_like(top, -1e30)
    acc5[...] = jnp.zeros_like(acc5)
    top5[...] = jnp.full_like(top5, -1e30)
    vt[HEAD_DIM:, :] = jnp.ones((vt.shape[0] - HEAD_DIM, vt.shape[1]), vt.dtype)
    vt5[HEAD_DIM:, :] = jnp.ones((vt5.shape[0] - HEAD_DIM, vt5.shape[1]), vt5.dtype)

    def forward(s):
        await_bytes(kv.at[s, :, 0], kv_sem.at[s])
        for r in range(1, side):
            remote(kv.at[s, :, 0], kv.at[s, :, r], fwd_sent.at[s], fwd_sem.at[s],
                   dev(a, minus(b, r, side), z)).start()

    forward(0)
    await_bytes(q5.at[0], q5_sem)
    for r in range(1, side):
        remote(q5.at[0], q5.at[r], q5f_sent, q5f_sem, dev(minus(a, r, side), b, z)).start()
    await_bytes(qm, q_sem)
    await_bytes(q5.at[pl.ds(1, side - 1)], q5f_sem)

    def absorb(keys, values_t, tiles, total, largest):
        scores = [nt(keys, tile) for tile in tiles]
        width = queries // len(tiles)
        for index, score in enumerate(scores):
            at = pl.ds(index * width, width)
            old = largest[:, at]
            new = jnp.maximum(old, jnp.max(score, axis=0, keepdims=True))
            weights = jnp.exp2((score - new) * EXP2_SCALE).astype(jnp.bfloat16)
            factor = jnp.exp2((old - new) * EXP2_SCALE)
            total[:, at] = total[:, at] * factor + jnp.dot(
                values_t, weights, preferred_element_type=jnp.float32
            )
            largest[:, at] = new

    tiles = max(1, queries // 1024)
    tile_r = side // tiles

    def step(i, _):
        s = order(i)

        @pl.when(i + LOOKAHEAD < nz)
        def _():
            forward(order(i + LOOKAHEAD))

        await_bytes(kv.at[s, :, pl.ds(1, side - 1)], fwd_sem.at[s])
        keys = kv[s, 0, :, :side].reshape(side * side * rows, HEAD_DIM)
        vt[:HEAD_DIM, :] = kv[s, 1, :, :side].reshape(side * side * rows, HEAD_DIM).T
        keys5 = kv[s, 0, :, side].reshape(side * rows, HEAD_DIM)
        vt5[:HEAD_DIM, :] = kv[s, 1, :, side].reshape(side * rows, HEAD_DIM).T
        own = [qm[t * tile_r:(t + 1) * tile_r].reshape(tile_r * block, HEAD_DIM) for t in range(tiles)]
        own5 = [q5[t * tile_r:(t + 1) * tile_r].reshape(tile_r * block, HEAD_DIM) for t in range(tiles)]
        absorb(keys, vt[...], own, acc, top)
        absorb(keys5, vt5[...], own5, acc5, top5)
        return 0

    for i in range(1, LOOKAHEAD):
        forward(order(jnp.int32(i)))
    lax.fori_loop(0, nz, step, 0)

    for r in range(side):
        a_ = plus(a, r, side)
        at = pl.ds(r * block, block)
        sums = acc5[HEAD_DIM:HEAD_DIM + 1, at]
        part = (acc5[:HEAD_DIM, at] / sums).astype(jnp.bfloat16)
        log_sum = jnp.broadcast_to(top5[:, at] * EXP2_SCALE + jnp.log2(sums), (8, block))
        for h in range(2):
            p_send[r, h] = part[:, h * group:(h + 1) * group]
            l_send[r, h] = log_sum[:, h * group:(h + 1) * group]
        own = acc[:HEAD_DIM, at] / acc[HEAD_DIM:HEAD_DIM + 1, at]
        o_send[r] = own.T.astype(jnp.bfloat16).reshape(2, group, HEAD_DIM)
        for h in range(2):
            moves = (
                (p_send.at[r, h], p_got.at[c, r], p_sent, p_sem),
                (l_send.at[r, h], l_got.at[c, r], l_sent, l_sem),
                (o_send.at[r, h], o_got.at[c, a], o_sent, o_sem),
            )

            def send():
                for src, dst, sent, got in moves:
                    remote(src, dst, sent, got, dev(a_, b, z, h)).start()

            def keep():
                for src, dst, sent, got in moves:
                    pltpu.make_async_copy(src, dst, got).start()

            if r:
                send()
            else:
                pl.when(c == h)(keep)
                pl.when(c != h)(send)

    def guided(conditional, unconditional):
        return unconditional + guidance_scale * (conditional - unconditional)

    await_bytes(p_got, p_sem)
    await_bytes(l_got, l_sem)
    joined = []
    for branch in range(2):
        log_sums = [l_got[branch, r][:1] for r in range(side)]
        largest = functools.reduce(jnp.maximum, log_sums)
        shares = [jnp.exp2(value - largest) for value in log_sums]
        total = sum(shares)
        joined.append(
            sum(p_got[branch, r].astype(jnp.float32) * (shares[r] / total) for r in range(side))
        )
    merged[:, side * HEAD_DIM:] = guided(*joined).T.astype(jnp.bfloat16)
    await_bytes(o_got, o_sem)
    for head in range(side):
        merged[:, head * HEAD_DIM:(head + 1) * HEAD_DIM] = guided(
            o_got[0, head].astype(jnp.float32), o_got[1, head].astype(jnp.float32)
        ).astype(jnp.bfloat16)

    width = heads * HEAD_DIM
    target = lax.div(z, half)
    place = out_ref.at[:, pl.ds(pl.multiple_of(lax.rem(z, half) * width, HEAD_DIM), width)]
    for j in range(half):
        s = c * half + j
        src = merged.at[pl.ds(j * rows, rows)]

        def send():
            remote(src, place, out_sent.at[j], out_sem, chip(x, y, plus(z, s, nz), target)).start()

        def keep():
            pltpu.make_async_copy(src, place, out_sem).start()

        if j:
            send()
        else:
            at_home = (c == 0) & (target == 0)
            pl.when(at_home)(keep)
            pl.when(jnp.logical_not(at_home))(send)

    await_bytes(kv.at[0, 0, 0, pl.ds(1, side - 1)], q_sent.at[0])
    await_bytes(kv.at[0, :, 0, pl.ds(1, side - 1)], kv_sent.at[0])

    def sent_layer(s, _):
        await_bytes(kv.at[s, 0, 0], q_sent.at[s])
        await_bytes(kv.at[s, :, 0], kv_sent.at[s])
        return 0

    lax.fori_loop(1, nz, sent_layer, 0)

    def sent_forward(s, _):
        await_bytes(kv.at[s, :, pl.ds(1, side - 1)], fwd_sent.at[s])
        return 0

    lax.fori_loop(0, nz, sent_forward, 0)
    await_bytes(q5.at[pl.ds(1, side - 1)], q5f_sent)
    for buffer, sem in ((p_send, p_sent), (l_send, l_sent), (o_send, o_sent)):
        await_bytes(buffer.at[pl.ds(1, side - 1)], sem)
        await_bytes(buffer.at[0, 0], sem)
    for j in range(half):
        src = merged.at[pl.ds(j * rows, rows)]
        if j:
            await_bytes(src, out_sent.at[j])
        else:
            pl.when(jnp.logical_not((c == 0) & (target == 0)))(
                lambda: await_bytes(src, out_sent.at[0])
            )
    await_bytes(out_ref, out_sem)


def on_device(queries, keys, values, latent, previous_velocity):
    nz = lax.axis_size("blk") // 2
    side = math.isqrt(lax.axis_size("uly") * 2)
    rows = queries.shape[1]
    columns = queries.shape[2] // 2
    heads = side + 1
    group = nz // 2 * rows
    count = side * nz * rows
    pad = 16
    dma = pltpu.SemaphoreType.DMA
    bf16, f32 = jnp.bfloat16, jnp.float32
    moved = pl.pallas_call(
        functools.partial(kernel, nz, side, rows),
        out_shape=jax.ShapeDtypeStruct((rows, columns), bf16),
        in_specs=[pl.BlockSpec(memory_space=pl.ANY)] * 3,
        out_specs=pl.BlockSpec(memory_space=pl.ANY),
        scratch_shapes=[
            pltpu.VMEM((nz, 2, side, heads, rows, HEAD_DIM), bf16),
            pltpu.VMEM((side, nz, rows, HEAD_DIM), bf16),
            pltpu.VMEM((side, nz, rows, HEAD_DIM), bf16),
            pltpu.VMEM((HEAD_DIM + pad, side * side * rows), bf16),
            pltpu.VMEM((HEAD_DIM + pad, side * rows), bf16),
            pltpu.VMEM((HEAD_DIM + pad, count), f32),
            pltpu.VMEM((1, count), f32),
            pltpu.VMEM((HEAD_DIM + pad, count), f32),
            pltpu.VMEM((1, count), f32),
            pltpu.VMEM((side, 2, group, HEAD_DIM), bf16),
            pltpu.VMEM((side, 2, HEAD_DIM, group), bf16),
            pltpu.VMEM((side, 2, 8, group), f32),
            pltpu.VMEM((2, side, group, HEAD_DIM), bf16),
            pltpu.VMEM((2, side, HEAD_DIM, group), bf16),
            pltpu.VMEM((2, side, 8, group), f32),
            pltpu.VMEM((group, heads * HEAD_DIM), bf16),
            dma, dma, dma, dma((nz,)), dma((nz,)), dma, dma, dma, dma,
            dma((nz,)), dma((nz,)), dma, dma((nz,)), dma, dma, dma, dma((nz // 2,)),
        ],
        compiler_params=pltpu.CompilerParams(
            collective_id=0, has_side_effects=True, vmem_limit_bytes=56 * 2**20
        ),
    )(queries, keys, values)
    velocity = moved.astype(jnp.float32)
    latent_next = latent + step_size * (1.5 * velocity - 0.5 * previous_velocity)
    return (velocity, latent_next)


def solution(mesh):
    in_specs = (
        P("cfg", ("blk", "uly"), None),
        P("cfg", ("blk", "uly"), None),
        P("cfg", ("blk", "uly"), None),
        P(("blk", "uly"), "cfg"),
        P(("blk", "uly"), "cfg"),
    )
    out_specs = (P(("blk", "uly"), "cfg"), P(("blk", "uly"), "cfg"))
    return jax.shard_map(
        on_device, mesh=mesh, in_specs=in_specs, out_specs=out_specs, check_vma=False
    )
```

```python
import functools
import math

import jax
import jax.numpy as jnp
from jax import lax
from jax.experimental import pallas as pl
from jax.experimental.pallas import tpu as pltpu
from jax.sharding import PartitionSpec as P

HEAD_DIM = 128

guidance_scale = 5.0
step_size = 0.25

EXP2_SCALE = math.log2(math.e) / math.sqrt(HEAD_DIM)
MESH = pl.DeviceIdType.MESH
AHEAD = 8
MERGE_AT = 2
EARLY_KV = 1
LATE = 1


def nt(left, right):
    return lax.dot_general(
        left, right, (((1,), (1,)), ((), ())), preferred_element_type=jnp.float32
    )


def kernel(
    nz, side, rows,
    q_ref, k_ref, v_ref, out_ref,
    line, kv, kv5, qm, q5, vt, vt5, acc, top, acc5, top5,
    o_send, p_send, l_send, o_got, p_got, l_got, merged,
    line_sem, q_sem, q5_sem, kv5_sem, q5f_sem, kv5f_sem, kv_sem, fwd_sem, across_sem, o_sem, p_sem, l_sem, out_sem,
    line_sent, q_sent, q5_sent, kv5_sent, q5f_sent, kv5f_sent, kv_sent, fwd_sent, across_sent,
    o_sent, p_sent, l_sent, out_sent, out5_sent,
):
    heads = side + 1
    half = nz // 2
    group = half * rows
    block = nz * rows
    queries = side * block
    tiles = (0, 1, 3, 2) if half == 4 else tuple(range(half))
    early, late = tiles[:half - LATE], tiles[half - LATE:]
    c = lax.axis_index("cfg")
    blk = lax.axis_index("blk")
    uly = lax.axis_index("uly")
    z = lax.div(blk, 2)
    x = lax.div(uly, side) * 2 + lax.rem(blk, 2)
    y = lax.rem(uly, side)
    a = x * (1 - c) + y * c
    b = y * (1 - c) + x * c

    def chip(x_, y_, z_, core):
        return (core, z_ * 2 + lax.rem(x_, 2), lax.div(x_, 2) * side + y_)

    def dev(a_, b_, z_, core=None):
        return chip(a_ * (1 - c) + b_ * c, b_ * (1 - c) + a_ * c, z_, c if core is None else core)

    def minus(value, steps, count):
        return lax.rem(value + count - steps, count)

    def plus(value, steps, count):
        return lax.rem(value + steps, count)

    def remote(src, dst, sent, got, device):
        return pltpu.make_async_remote_copy(
            src_ref=src, dst_ref=dst, send_sem=sent, recv_sem=got,
            device_id=device, device_id_type=MESH,
        )

    def await_bytes(ref, sem):
        pltpu.make_async_copy(ref, ref, sem).wait()

    barrier = pltpu.get_barrier_semaphore()

    def greet(device):
        pl.semaphore_signal(barrier, inc=1, device_id=device, device_id_type=MESH)

    def greet_layer(s, _):
        z_ = minus(z, s, nz)
        for r in range(side):
            greet(dev(minus(a, r, side), b, z_))
        greet(chip(x, y, z_, 1 - c))
        return 0

    for r in range(1, side):
        greet(dev(minus(a, r, side), b, z))
        greet(dev(a, minus(b, r, side), z))
        greet(chip(minus(x, r, side), y, z, 1 - c))
        greet(chip(x, minus(y, r, side), z, 1 - c))
    greet(chip(x, y, z, 1 - c))
    lax.fori_loop(1, nz, greet_layer, 0)
    pl.semaphore_wait(barrier, 4 * (side - 1) + 1 + (nz - 1) * (side + 1))

    others = pl.ds(1, side - 1)

    def cols(z_, head):
        return pl.ds(pl.multiple_of((z_ * heads + head) * HEAD_DIM, HEAD_DIM), HEAD_DIM)

    def order(i):
        odd = lax.rem(i, 2)
        later = lax.div(i, 2) + half * jnp.minimum(i, 1)
        return odd * lax.div(i + 1, 2) + (1 - odd) * later

    shared = (
        (q_ref, lambda s: q5.at[0, s], q5_sent, q5_sem),
        (k_ref, lambda s: kv5.at[0, 0, s], kv5_sent, kv5_sem),
        (v_ref, lambda s: kv5.at[1, 0, s], kv5_sent, kv5_sem),
    )

    def send_shared(i, _):
        s = order(i)
        z_ = minus(z, s, nz)
        for ref, place, sent, got in shared:
            remote(ref.at[0, :, cols(z_, side)], place(s), sent, got, dev(a, b, z_)).start()
        return 0

    def gather_line(part, s):
        ref = (q_ref, k_ref, v_ref)[part]
        z_ = minus(z, s, nz)
        first = isinstance(s, int) and s == 0
        if first:
            place = qm.at[0, 0] if part == 0 else kv.at[0, part - 1, 0]
            got = q_sem.at[0] if part == 0 else kv_sem.at[0]
        else:
            place = line.at[part, s]
            got = line_sem.at[part, s]
        pltpu.make_async_copy(ref.at[0, :, cols(z_, a)], place.at[0], got).start()
        for r in range(1, side):
            a_ = minus(a, r, side)
            remote(ref.at[0, :, cols(z_, a_)], place.at[r], line_sent.at[part], got,
                   dev(a_, b, z)).start()

    def gather_q(i, _):
        gather_line(0, order(i))
        return 0

    def gather_kv(i, _):
        gather_line(1, order(i))
        gather_line(2, order(i))
        return 0

    def send_q(t):
        for h in range(2):
            s = t + h * half
            if s:
                await_bytes(line.at[0, s], line_sem.at[0, s])
                remote(line.at[0, s], qm.at[t, h], q_sent.at[t, h], q_sem.at[t],
                       dev(a, b, minus(z, s, nz))).start()

    def sent_q(t):
        for h in range(2):
            if t or h:
                await_bytes(qm.at[t, h], q_sent.at[t, h])

    def send_kv(s):
        for part in range(2):
            await_bytes(line.at[part + 1, s], line_sem.at[part + 1, s])
            remote(line.at[part + 1, s], kv.at[s, part, 0], kv_sent.at[s], kv_sem.at[s],
                   dev(a, b, minus(z, s, nz))).start()

    def send_kv_layer(i, _):
        send_kv(order(i))
        return 0

    near = sorted({1, side - 1})
    across = side == 4

    def forward(s):
        await_bytes(kv.at[s, :, 0], kv_sem.at[s])
        for index, r in enumerate(near):
            remote(kv.at[s, :, 0], kv.at[s, :, r], fwd_sent.at[s, index], fwd_sem.at[s, index],
                   dev(a, minus(b, r, side), z)).start()

    def relay(s):
        for index, r in enumerate(near):
            await_bytes(kv.at[s, :, r], fwd_sem.at[s, index])
            if across:
                remote(kv.at[s, index, r], kv.at[s, index, 2], across_sent.at[s], across_sem.at[s],
                       dev(a, minus(b, r, side), z)).start()

    for ref, place, sent, got in shared:
        pltpu.make_async_copy(ref.at[0, :, cols(z, side)], place(0), got).start()
    lax.fori_loop(1, nz, send_shared, 0)
    gather_line(0, 0)
    lax.fori_loop(1, nz, gather_q, 0)
    gather_line(1, 0)
    gather_line(2, 0)
    lax.fori_loop(1, nz, gather_kv, 0)

    acc[...] = jnp.zeros_like(acc)
    top[...] = jnp.full_like(top, -1e30)
    acc5[...] = jnp.zeros_like(acc5)
    top5[...] = jnp.full_like(top5, -1e30)
    vt5[HEAD_DIM:, :] = jnp.ones((vt5.shape[0] - HEAD_DIM, vt5.shape[1]), vt5.dtype)
    for s in range(nz):
        vt[s, HEAD_DIM:, :] = jnp.ones((vt.shape[1] - HEAD_DIM, vt.shape[2]), vt.dtype)

    layers = pl.ds(1, nz - 1)
    await_bytes(q5.at[0, layers], q5_sent)
    await_bytes(kv5.at[:, 0, layers], kv5_sent)
    for t in early:
        send_q(t)

    await_bytes(q5.at[0], q5_sem)
    for r in range(1, side):
        remote(q5.at[0], q5.at[r], q5f_sent, q5f_sem, dev(minus(a, r, side), b, z)).start()
    await_bytes(kv5.at[:, 0], kv5_sem)
    for r in range(1, side):
        remote(kv5.at[:, 0], kv5.at[:, r], kv5f_sent, kv5f_sem, dev(a, minus(b, r, side), z)).start()

    lax.fori_loop(1, min(EARLY_KV, nz), send_kv_layer, 0)
    for t in early:
        sent_q(t)
    lax.fori_loop(min(EARLY_KV, nz), min(AHEAD, nz), send_kv_layer, 0)

    def weigh(score, peak):
        return jnp.exp2((score - peak) * EXP2_SCALE).astype(jnp.bfloat16)

    def absorb(keys, values_t, parts, wide, rows_ref, total, largest, then=None):
        scores = [nt(keys, rows_ref[t].reshape(wide, HEAD_DIM)) for t in parts]
        for t, score in zip(parts, scores):
            at = pl.ds(t * wide, wide)
            old = largest[:, at]
            new = jnp.maximum(old, jnp.max(score, axis=0, keepdims=True))
            factor = jnp.exp2((old - new) * EXP2_SCALE)
            total[:, at] = total[:, at] * factor + jnp.dot(
                values_t[...], weigh(score, new), preferred_element_type=jnp.float32
            )
            largest[:, at] = new
            if then is not None:
                then(t, total[:, at])

    span = side * side * rows
    tile = 2 * side * rows
    chunks = nz // side
    split = side // chunks

    def absorb_shared(i, _):
        at = pl.ds(i * split, split)
        vt5[:HEAD_DIM, :] = kv5[1, at].reshape(span, HEAD_DIM).T
        absorb(kv5[0, at].reshape(span, HEAD_DIM), vt5, range(side), block, q5, acc5, top5)
        return 0

    await_bytes(q5.at[others], q5f_sem)
    await_bytes(kv5.at[:, others], kv5f_sem)
    forward(0)
    absorb_shared(0, 0)
    forward(order(jnp.int32(1)))
    relay(0)
    lax.fori_loop(1, chunks, absorb_shared, 0)

    def spread(r, moves):
        for h in range(2):
            def send():
                for src, dst, sent, got in moves(h):
                    remote(src, dst, sent, got, dev(plus(a, r, side), b, z, h)).start()

            def keep():
                for src, dst, sent, got in moves(h):
                    pltpu.make_async_copy(src, dst, got).start()

            if r:
                send()
            else:
                pl.when(c == h)(keep)
                pl.when(c != h)(send)

    for r in range(side):
        at = pl.ds(r * block, block)
        sums = acc5[HEAD_DIM:HEAD_DIM + 1, at]
        part = (acc5[:HEAD_DIM, at] / sums).astype(jnp.bfloat16)
        log_sum = jnp.broadcast_to(top5[:, at] * EXP2_SCALE + jnp.log2(sums), (8, block))
        for h in range(2):
            p_send[r, h] = part[:, h * group:(h + 1) * group]
            l_send[r, h] = log_sum[:, h * group:(h + 1) * group]
        spread(r, lambda h: (
            (p_send.at[r, h], p_got.at[c, r], p_sent, p_sem),
            (l_send.at[r, h], l_got.at[c, r], l_sent, l_sem),
        ))

    def guided(conditional, unconditional):
        return unconditional + guidance_scale * (conditional - unconditional)

    width = heads * HEAD_DIM
    target = lax.div(z, half)
    at_home = (c == 0) & (target == 0)

    def deliver(first, count, sent, *slots):
        start = pl.multiple_of(lax.rem(z, half) * width + first * HEAD_DIM, HEAD_DIM)
        place = out_ref.at[:, pl.ds(start, count * HEAD_DIM)]
        for j in slots or range(half):
            src = merged.at[pl.ds(j * rows, rows), pl.ds(first * HEAD_DIM, count * HEAD_DIM)]

            def send():
                remote(src, place, sent.at[j], out_sem,
                       chip(x, y, plus(z, c * half + j, nz), target)).start()

            def keep():
                pltpu.make_async_copy(src, place, out_sem).start()

            if j:
                send()
            else:
                pl.when(at_home)(keep)
                pl.when(jnp.logical_not(at_home))(send)

    def delivered(first, count, sent):
        for j in range(half):
            src = merged.at[pl.ds(j * rows, rows), pl.ds(first * HEAD_DIM, count * HEAD_DIM)]
            if j:
                await_bytes(src, sent.at[j])
            else:
                pl.when(jnp.logical_not(at_home))(lambda: await_bytes(src, sent.at[0]))

    def merge_shared():
        await_bytes(p_got, p_sem)
        await_bytes(l_got, l_sem)
        joined = []
        for branch in range(2):
            log_sums = [l_got[branch, r][:1] for r in range(side)]
            largest = functools.reduce(jnp.maximum, log_sums)
            shares = [jnp.exp2(value - largest) for value in log_sums]
            total = sum(shares)
            joined.append(
                sum(p_got[branch, r].astype(jnp.float32) * (shares[r] / total) for r in range(side))
            )
        merged[:, side * HEAD_DIM:] = guided(*joined).T.astype(jnp.bfloat16)
        deliver(side, 1, out5_sent)

    for t in early:
        await_bytes(qm.at[t], q_sem.at[t])

    def step(i, then):
        s = order(i)
        await_bytes(kv.at[s, :, 2], across_sem.at[s]) if across else None
        vt[s, :HEAD_DIM, :] = kv[s, 1].reshape(span, HEAD_DIM).T
        absorb(kv[s, 0].reshape(span, HEAD_DIM), vt.at[s], early, tile, qm, acc, top, then)

    def prepared_step(i, _):
        @pl.when(i + AHEAD < nz)
        def _():
            send_kv_layer(i + AHEAD, 0)

        @pl.when(i == max(nz - AHEAD, 0))
        def _():
            for t in late:
                send_q(t)

        @pl.when(i + 2 < nz)
        def _():
            forward(order(i + 2))

        relay(order(i + 1))
        pl.when(i == MERGE_AT)(merge_shared)
        step(i, None)
        return 0

    def finish(t, total):
        own = (total[:HEAD_DIM] / total[HEAD_DIM:HEAD_DIM + 1]).T
        o_send[t] = own.astype(jnp.bfloat16).reshape(2, side, rows, HEAD_DIM)
        for r in range(side):
            spread(r, lambda h: ((o_send.at[t, h, r], o_got.at[t, c, a], o_sent.at[t], o_sem.at[t]),))

    def merge(t):
        await_bytes(o_got.at[t], o_sem.at[t])
        for head in range(side):
            merged[t * rows:(t + 1) * rows, head * HEAD_DIM:(head + 1) * HEAD_DIM] = guided(
                o_got[t, 0, head].astype(jnp.float32), o_got[t, 1, head].astype(jnp.float32)
            ).astype(jnp.bfloat16)
        deliver(0, side, out_sent, t)

    lax.fori_loop(0, nz - 1, prepared_step, 0)
    step(jnp.int32(nz - 1), finish)

    def attend(t):
        own = qm[t].reshape(tile, HEAD_DIM)

        def score(s):
            return nt(kv[s, 0].reshape(span, HEAD_DIM), own)

        pairs = [(s, s + 1) for s in range(0, nz, 2)]
        ready = [score(s) for s in pairs[0]]
        peak = jnp.full((1, tile), -1e30, jnp.float32)
        total = jnp.zeros((vt.shape[1], tile), jnp.float32)
        for index, pair in enumerate(pairs):
            following = [score(s) for s in pairs[index + 1]] if index + 1 < len(pairs) else None
            new = peak
            for value in ready:
                new = jnp.maximum(new, jnp.max(value, axis=0, keepdims=True))
            total = total * jnp.exp2((peak - new) * EXP2_SCALE)
            for s, value in zip(pair, ready):
                total = total + jnp.dot(vt[s], weigh(value, new), preferred_element_type=jnp.float32)
            peak, ready = new, following
        finish(t, total)

    waiting = list(early)
    for t in late:
        await_bytes(qm.at[t], q_sem.at[t])
        attend(t)
        for done in waiting:
            merge(done)
        waiting = [t]
    for done in waiting:
        merge(done)

    for part in range(3):
        await_bytes(line.at[part, :, others], line_sent.at[part])

    def sent_layer(s, _):
        await_bytes(kv.at[s, :, 0], kv_sent.at[s])
        return 0

    lax.fori_loop(1, nz, sent_layer, 0)

    def sent_forward(s, _):
        for index, r in enumerate(near):
            await_bytes(kv.at[s, :, r], fwd_sent.at[s, index])
        if across:
            await_bytes(kv.at[s, :, 2], across_sent.at[s])
        return 0

    lax.fori_loop(0, nz, sent_forward, 0)
    await_bytes(q5.at[others], q5f_sent)
    await_bytes(kv5.at[:, others], kv5f_sent)
    for buffer, sem in ((p_send, p_sent), (l_send, l_sent)):
        await_bytes(buffer.at[others], sem)
        await_bytes(buffer.at[0, 0], sem)
    for t in range(half):
        await_bytes(o_send.at[t, :, others], o_sent.at[t])
        await_bytes(o_send.at[t, 0, 0], o_sent.at[t])
    for t in late:
        sent_q(t)
    delivered(side, 1, out5_sent)
    delivered(0, side, out_sent)
    await_bytes(out_ref, out_sem)


def on_device(queries, keys, values, latent, previous_velocity):
    nz = lax.axis_size("blk") // 2
    side = math.isqrt(lax.axis_size("uly") * 2)
    rows = queries.shape[1]
    columns = queries.shape[2] // 2
    heads = side + 1
    group = nz // 2 * rows
    count = side * nz * rows
    pad = 16
    dma = pltpu.SemaphoreType.DMA
    bf16, f32 = jnp.bfloat16, jnp.float32
    moved = pl.pallas_call(
        functools.partial(kernel, nz, side, rows),
        out_shape=jax.ShapeDtypeStruct((rows, columns), bf16),
        in_specs=[pl.BlockSpec(memory_space=pl.ANY)] * 3,
        out_specs=pl.BlockSpec(memory_space=pl.ANY),
        scratch_shapes=[
            pltpu.VMEM((3, nz, side, rows, HEAD_DIM), bf16),
            pltpu.VMEM((nz, 2, side, side, rows, HEAD_DIM), bf16),
            pltpu.VMEM((2, side, nz, rows, HEAD_DIM), bf16),
            pltpu.VMEM((nz // 2, 2, side, rows, HEAD_DIM), bf16),
            pltpu.VMEM((side, nz, rows, HEAD_DIM), bf16),
            pltpu.VMEM((nz, HEAD_DIM + pad, side * side * rows), bf16),
            pltpu.VMEM((HEAD_DIM + pad, side * side * rows), bf16),
            pltpu.VMEM((HEAD_DIM + pad, count), f32),
            pltpu.VMEM((1, count), f32),
            pltpu.VMEM((HEAD_DIM + pad, count), f32),
            pltpu.VMEM((1, count), f32),
            pltpu.VMEM((nz // 2, 2, side, rows, HEAD_DIM), bf16),
            pltpu.VMEM((side, 2, HEAD_DIM, group), bf16),
            pltpu.VMEM((side, 2, 8, group), f32),
            pltpu.VMEM((nz // 2, 2, side, rows, HEAD_DIM), bf16),
            pltpu.VMEM((2, side, HEAD_DIM, group), bf16),
            pltpu.VMEM((2, side, 8, group), f32),
            pltpu.VMEM((group, heads * HEAD_DIM), bf16),
            dma((3, nz)), dma((nz // 2,)), dma, dma, dma, dma, dma((nz,)), dma((nz, 2)), dma((nz,)),
            dma((nz // 2,)), dma, dma, dma,
            dma((3,)), dma((nz // 2, 2)), dma, dma, dma, dma, dma((nz,)), dma((nz, 2)), dma((nz,)),
            dma((nz // 2,)), dma, dma, dma((nz // 2,)), dma((nz // 2,)),
        ],
        compiler_params=pltpu.CompilerParams(
            collective_id=0, has_side_effects=True, vmem_limit_bytes=56 * 2**20
        ),
    )(queries, keys, values)
    velocity = moved.astype(jnp.float32)
    latent_next = latent + step_size * (1.5 * velocity - 0.5 * previous_velocity)
    return (velocity, latent_next)


def solution(mesh):
    in_specs = (
        P("cfg", ("blk", "uly"), None),
        P("cfg", ("blk", "uly"), None),
        P("cfg", ("blk", "uly"), None),
        P(("blk", "uly"), "cfg"),
        P(("blk", "uly"), "cfg"),
    )
    out_specs = (P(("blk", "uly"), "cfg"), P(("blk", "uly"), "cfg"))
    return jax.shard_map(
        on_device, mesh=mesh, in_specs=in_specs, out_specs=out_specs, check_vma=False
    )
```

```python
import functools
import math

import jax
import jax.numpy as jnp
from jax import lax
from jax.experimental import pallas as pl
from jax.experimental.pallas import tpu as pltpu
from jax.sharding import PartitionSpec as P

HEAD_DIM = 128

guidance_scale = 5.0
step_size = 0.25

EXP2_SCALE = math.log2(math.e) / math.sqrt(HEAD_DIM)
MESH = pl.DeviceIdType.MESH
MERGE_AT = 5
LATE = 1
CATCH_UP = 2
BEFORE = 4


def nt(left, right):
    return lax.dot_general(
        left, right, (((1,), (1,)), ((), ())), preferred_element_type=jnp.float32
    )


def kernel(
    nz, side, rows,
    q_ref, k_ref, v_ref, out_ref,
    line, kv, kv5, qm, q5, vt, vt5, acc, top, acc5, top5,
    o_send, p_send, l_send, o_got, p_got, l_got, merged,
    line_sem, q_sem, q5_sem, kv5_sem, q5f_sem, kv5f_sem, kv_sem, fwd_sem, o_sem, p_sem, l_sem, out_sem,
    line_sent, q_sent, q5_sent, kv5_sent, q5f_sent, kv5f_sent, kv_sent, fwd_sent,
    o_sent, p_sent, l_sent, out_sent, out5_sent,
):
    heads = side + 1
    half = nz // 2
    group = half * rows
    block = nz * rows
    queries = side * block
    tiles = (0, 1, 3, 2) if half == 4 else tuple(range(half))
    early, late = tiles[:half - LATE], tiles[half - LATE:]
    c = lax.axis_index("cfg")
    blk = lax.axis_index("blk")
    uly = lax.axis_index("uly")
    z = lax.div(blk, 2)
    x = lax.div(uly, side) * 2 + lax.rem(blk, 2)
    y = lax.rem(uly, side)
    a = x * (1 - c) + y * c
    b = y * (1 - c) + x * c

    def chip(x_, y_, z_, core):
        return (core, z_ * 2 + lax.rem(x_, 2), lax.div(x_, 2) * side + y_)

    def dev(a_, b_, z_, core=None):
        return chip(a_ * (1 - c) + b_ * c, b_ * (1 - c) + a_ * c, z_, c if core is None else core)

    def minus(value, steps, count):
        return lax.rem(value + count - steps, count)

    def plus(value, steps, count):
        return lax.rem(value + steps, count)

    def remote(src, dst, sent, got, device):
        return pltpu.make_async_remote_copy(
            src_ref=src, dst_ref=dst, send_sem=sent, recv_sem=got,
            device_id=device, device_id_type=MESH,
        )

    def await_bytes(ref, sem):
        pltpu.make_async_copy(ref, ref, sem).wait()

    barrier = pltpu.get_barrier_semaphore()

    def greet(device):
        pl.semaphore_signal(barrier, inc=1, device_id=device, device_id_type=MESH)

    def greet_layer(s, _):
        z_ = minus(z, s, nz)
        for r in range(side):
            greet(dev(minus(a, r, side), b, z_))
        greet(chip(x, y, z_, 1 - c))
        return 0

    for r in range(1, side):
        greet(dev(minus(a, r, side), b, z))
        greet(dev(a, minus(b, r, side), z))
        greet(chip(minus(x, r, side), y, z, 1 - c))
        greet(chip(x, minus(y, r, side), z, 1 - c))
    greet(chip(x, y, z, 1 - c))
    lax.fori_loop(1, nz, greet_layer, 0)
    pl.semaphore_wait(barrier, 4 * (side - 1) + 1 + (nz - 1) * (side + 1))

    others = pl.ds(1, side - 1)

    def cols(z_, head):
        return pl.ds(pl.multiple_of((z_ * heads + head) * HEAD_DIM, HEAD_DIM), HEAD_DIM)

    def order(i):
        odd = lax.rem(i, 2)
        later = lax.div(i, 2) + half * jnp.minimum(i, 1)
        return odd * lax.div(i + 1, 2) + (1 - odd) * later

    shared = (
        (q_ref, lambda s: q5.at[0, s], q5_sent, q5_sem),
        (k_ref, lambda s: kv5.at[0, 0, s], kv5_sent, kv5_sem),
        (v_ref, lambda s: kv5.at[1, 0, s], kv5_sent, kv5_sem),
    )

    def send_shared(i, _):
        s = order(i)
        z_ = minus(z, s, nz)
        for ref, place, sent, got in shared:
            remote(ref.at[0, :, cols(z_, side)], place(s), sent, got, dev(a, b, z_)).start()
        return 0

    def gather_line(part, s):
        ref = (q_ref, k_ref, v_ref)[part]
        z_ = minus(z, s, nz)
        first = isinstance(s, int) and s == 0
        if first:
            place = qm.at[0, 0] if part == 0 else kv.at[0, part - 1, 0]
            got = q_sem.at[0] if part == 0 else kv_sem.at[0]
        else:
            place = line.at[part, s]
            got = line_sem.at[part, s]
        pltpu.make_async_copy(ref.at[0, :, cols(z_, a)], place.at[0], got).start()
        for r in range(1, side):
            a_ = minus(a, r, side)
            remote(ref.at[0, :, cols(z_, a_)], place.at[r], line_sent.at[part], got,
                   dev(a_, b, z)).start()

    def gather_q(i, _):
        gather_line(0, order(i))
        return 0

    def gather_kv(i, _):
        gather_line(1, order(i))
        gather_line(2, order(i))
        return 0

    def send_q(t):
        for h in range(2):
            s = t + h * half
            if s:
                await_bytes(line.at[0, s], line_sem.at[0, s])
                remote(line.at[0, s], qm.at[t, h], q_sent.at[t, h], q_sem.at[t],
                       dev(a, b, minus(z, s, nz))).start()

    def sent_q(t):
        for h in range(2):
            if t or h:
                await_bytes(qm.at[t, h], q_sent.at[t, h])

    def send_kv(s):
        for part in range(2):
            await_bytes(line.at[part + 1, s], line_sem.at[part + 1, s])
            remote(line.at[part + 1, s], kv.at[s, part, 0], kv_sent.at[s], kv_sem.at[s],
                   dev(a, b, minus(z, s, nz))).start()

    def send_kv_layer(i, _):
        send_kv(order(i))
        return 0

    def forward(s):
        await_bytes(kv.at[s, :, 0], kv_sem.at[s])
        for r in (2, 1, 3)[:side - 1] if side > 2 else (1,):
            remote(kv.at[s, :, 0], kv.at[s, :, r], fwd_sent.at[s], fwd_sem.at[s],
                   dev(a, minus(b, r, side), z)).start()

    for ref, place, sent, got in shared:
        pltpu.make_async_copy(ref.at[0, :, cols(z, side)], place(0), got).start()
    lax.fori_loop(1, nz, send_shared, 0)
    gather_line(0, 0)
    lax.fori_loop(1, nz, gather_q, 0)
    gather_line(1, 0)
    gather_line(2, 0)
    lax.fori_loop(1, nz, gather_kv, 0)

    acc[...] = jnp.zeros_like(acc)
    top[...] = jnp.full_like(top, -1e30)
    acc5[...] = jnp.zeros_like(acc5)
    top5[...] = jnp.full_like(top5, -1e30)
    vt5[HEAD_DIM:, :] = jnp.ones((vt5.shape[0] - HEAD_DIM, vt5.shape[1]), vt5.dtype)
    for s in range(nz):
        vt[s, HEAD_DIM:, :] = jnp.ones((vt.shape[1] - HEAD_DIM, vt.shape[2]), vt.dtype)

    layers = pl.ds(1, nz - 1)
    await_bytes(q5.at[0, layers], q5_sent)
    await_bytes(kv5.at[:, 0, layers], kv5_sent)
    for t in early:
        send_q(t)

    await_bytes(q5.at[0], q5_sem)
    for r in range(1, side):
        remote(q5.at[0], q5.at[r], q5f_sent, q5f_sem, dev(minus(a, r, side), b, z)).start()
    await_bytes(kv5.at[:, 0], kv5_sem)
    for r in range(1, side):
        remote(kv5.at[:, 0], kv5.at[:, r], kv5f_sent, kv5f_sem, dev(a, minus(b, r, side), z)).start()

    for t in early:
        sent_q(t)
    lax.fori_loop(1, min(1 + BEFORE, nz), send_kv_layer, 0)
    for t in late:
        send_q(t)
    lax.fori_loop(min(1 + BEFORE, nz), nz, send_kv_layer, 0)

    def weigh(score, peak):
        return jnp.exp2((score - peak) * EXP2_SCALE).astype(jnp.bfloat16)

    def absorb(keys, values_t, parts, wide, rows_ref, total, largest, then=None):
        scores = [nt(keys, rows_ref[t].reshape(wide, HEAD_DIM)) for t in parts]
        for t, score in zip(parts, scores):
            at = pl.ds(t * wide, wide)
            old = largest[:, at]
            new = jnp.maximum(old, jnp.max(score, axis=0, keepdims=True))
            factor = jnp.exp2((old - new) * EXP2_SCALE)
            total[:, at] = total[:, at] * factor + jnp.dot(
                values_t[...], weigh(score, new), preferred_element_type=jnp.float32
            )
            largest[:, at] = new
            if then is not None:
                then(t, total[:, at])

    span = side * side * rows
    tile = 2 * side * rows
    chunks = nz // side
    split = side // chunks

    def absorb_shared(i, _):
        at = pl.ds(i * split, split)
        vt5[:HEAD_DIM, :] = kv5[1, at].reshape(span, HEAD_DIM).T
        absorb(kv5[0, at].reshape(span, HEAD_DIM), vt5, range(side), block, q5, acc5, top5)
        return 0

    await_bytes(q5.at[others], q5f_sem)
    await_bytes(kv5.at[:, others], kv5f_sem)
    forward(0)
    absorb_shared(0, 0)
    lax.fori_loop(1, chunks, absorb_shared, 0)

    def spread(r, moves):
        for h in range(2):
            def send():
                for src, dst, sent, got in moves(h):
                    remote(src, dst, sent, got, dev(plus(a, r, side), b, z, h)).start()

            def keep():
                for src, dst, sent, got in moves(h):
                    pltpu.make_async_copy(src, dst, got).start()

            if r:
                send()
            else:
                pl.when(c == h)(keep)
                pl.when(c != h)(send)

    for r in range(side):
        at = pl.ds(r * block, block)
        sums = acc5[HEAD_DIM:HEAD_DIM + 1, at]
        part = (acc5[:HEAD_DIM, at] / sums).astype(jnp.bfloat16)
        log_sum = jnp.broadcast_to(top5[:, at] * EXP2_SCALE + jnp.log2(sums), (8, block))
        for h in range(2):
            p_send[r, h] = part[:, h * group:(h + 1) * group]
            l_send[r, h] = log_sum[:, h * group:(h + 1) * group]
        spread(r, lambda h: (
            (p_send.at[r, h], p_got.at[c, r], p_sent, p_sem),
            (l_send.at[r, h], l_got.at[c, r], l_sent, l_sem),
        ))

    def guided(conditional, unconditional):
        return unconditional + guidance_scale * (conditional - unconditional)

    width = heads * HEAD_DIM
    target = lax.div(z, half)
    at_home = (c == 0) & (target == 0)

    def deliver(first, count, sent, *slots):
        start = pl.multiple_of(lax.rem(z, half) * width + first * HEAD_DIM, HEAD_DIM)
        place = out_ref.at[:, pl.ds(start, count * HEAD_DIM)]
        for j in slots or range(half):
            src = merged.at[pl.ds(j * rows, rows), pl.ds(first * HEAD_DIM, count * HEAD_DIM)]

            def send():
                remote(src, place, sent.at[j], out_sem,
                       chip(x, y, plus(z, c * half + j, nz), target)).start()

            def keep():
                pltpu.make_async_copy(src, place, out_sem).start()

            if j:
                send()
            else:
                pl.when(at_home)(keep)
                pl.when(jnp.logical_not(at_home))(send)

    def delivered(first, count, sent):
        for j in range(half):
            src = merged.at[pl.ds(j * rows, rows), pl.ds(first * HEAD_DIM, count * HEAD_DIM)]
            if j:
                await_bytes(src, sent.at[j])
            else:
                pl.when(jnp.logical_not(at_home))(lambda: await_bytes(src, sent.at[0]))

    def merge_shared():
        await_bytes(p_got, p_sem)
        await_bytes(l_got, l_sem)
        joined = []
        for branch in range(2):
            log_sums = [l_got[branch, r][:1] for r in range(side)]
            largest = functools.reduce(jnp.maximum, log_sums)
            shares = [jnp.exp2(value - largest) for value in log_sums]
            total = sum(shares)
            joined.append(
                sum(p_got[branch, r].astype(jnp.float32) * (shares[r] / total) for r in range(side))
            )
        merged[:, side * HEAD_DIM:] = guided(*joined).T.astype(jnp.bfloat16)
        deliver(side, 1, out5_sent)

    for t in early:
        await_bytes(qm.at[t], q_sem.at[t])

    def step(i, then):
        s = order(i)
        await_bytes(kv.at[s, :, others], fwd_sem.at[s])
        vt[s, :HEAD_DIM, :] = kv[s, 1].reshape(span, HEAD_DIM).T
        absorb(kv[s, 0].reshape(span, HEAD_DIM), vt.at[s], early, tile, qm, acc, top, then)

    def prepared_step(i, _):
        forward(order(i + 1))
        pl.when(i == MERGE_AT)(merge_shared)
        step(i, None)

        @pl.when(i == nz - CATCH_UP)
        def _():
            for t in late:
                await_bytes(qm.at[t], q_sem.at[t])
                attend(t, 0, half, False)

        return 0

    def finish(t, total):
        own = (total[:HEAD_DIM] / total[HEAD_DIM:HEAD_DIM + 1]).T
        o_send[t] = own.astype(jnp.bfloat16).reshape(2, side, rows, HEAD_DIM)
        for r in range(side):
            spread(r, lambda h: ((o_send.at[t, h, r], o_got.at[t, c, a], o_sent.at[t], o_sem.at[t]),))

    def merge(t):
        await_bytes(o_got.at[t], o_sem.at[t])
        for head in range(side):
            merged[t * rows:(t + 1) * rows, head * HEAD_DIM:(head + 1) * HEAD_DIM] = guided(
                o_got[t, 0, head].astype(jnp.float32), o_got[t, 1, head].astype(jnp.float32)
            ).astype(jnp.bfloat16)
        deliver(0, side, out_sent, t)


    sequence = [0] + [(i + 1) // 2 if i % 2 else i // 2 + half for i in range(1, nz)]

    def attend(t, first, stop, last):
        at = pl.ds(t * tile, tile)
        own = qm[t].reshape(tile, HEAD_DIM)

        def score(s):
            return nt(kv[s, 0].reshape(span, HEAD_DIM), own)

        pairs = [sequence[i:i + 2] for i in range(first, stop, 2)]
        ready = [score(s) for s in pairs[0]]
        peak, total = top[:, at], acc[:, at]
        for index, pair in enumerate(pairs):
            following = [score(s) for s in pairs[index + 1]] if index + 1 < len(pairs) else None
            new = peak
            for value in ready:
                new = jnp.maximum(new, jnp.max(value, axis=0, keepdims=True))
            total = total * jnp.exp2((peak - new) * EXP2_SCALE)
            for s, value in zip(pair, ready):
                total = total + jnp.dot(vt[s], weigh(value, new), preferred_element_type=jnp.float32)
            peak, ready = new, following
        if last:
            finish(t, total)
        else:
            acc[:, at], top[:, at] = total, peak

    lax.fori_loop(0, nz - 1, prepared_step, 0)
    step(jnp.int32(nz - 1), finish)

    waiting = list(early)
    for t in late:
        attend(t, half, nz, True)
        for done in waiting:
            merge(done)
        waiting = [t]
    for done in waiting:
        merge(done)

    for part in range(3):
        await_bytes(line.at[part, :, others], line_sent.at[part])

    def sent_layer(s, _):
        await_bytes(kv.at[s, :, 0], kv_sent.at[s])
        return 0

    lax.fori_loop(1, nz, sent_layer, 0)

    def sent_forward(s, _):
        await_bytes(kv.at[s, :, others], fwd_sent.at[s])
        return 0

    lax.fori_loop(0, nz, sent_forward, 0)
    await_bytes(q5.at[others], q5f_sent)
    await_bytes(kv5.at[:, others], kv5f_sent)
    for buffer, sem in ((p_send, p_sent), (l_send, l_sent)):
        await_bytes(buffer.at[others], sem)
        await_bytes(buffer.at[0, 0], sem)
    for t in range(half):
        await_bytes(o_send.at[t, :, others], o_sent.at[t])
        await_bytes(o_send.at[t, 0, 0], o_sent.at[t])
    for t in late:
        sent_q(t)
    delivered(side, 1, out5_sent)
    delivered(0, side, out_sent)
    await_bytes(out_ref, out_sem)


def on_device(queries, keys, values, latent, previous_velocity):
    nz = lax.axis_size("blk") // 2
    side = math.isqrt(lax.axis_size("uly") * 2)
    rows = queries.shape[1]
    columns = queries.shape[2] // 2
    heads = side + 1
    group = nz // 2 * rows
    count = side * nz * rows
    pad = 16
    dma = pltpu.SemaphoreType.DMA
    bf16, f32 = jnp.bfloat16, jnp.float32
    moved = pl.pallas_call(
        functools.partial(kernel, nz, side, rows),
        out_shape=jax.ShapeDtypeStruct((rows, columns), bf16),
        in_specs=[pl.BlockSpec(memory_space=pl.ANY)] * 3,
        out_specs=pl.BlockSpec(memory_space=pl.ANY),
        scratch_shapes=[
            pltpu.VMEM((3, nz, side, rows, HEAD_DIM), bf16),
            pltpu.VMEM((nz, 2, side, side, rows, HEAD_DIM), bf16),
            pltpu.VMEM((2, side, nz, rows, HEAD_DIM), bf16),
            pltpu.VMEM((nz // 2, 2, side, rows, HEAD_DIM), bf16),
            pltpu.VMEM((side, nz, rows, HEAD_DIM), bf16),
            pltpu.VMEM((nz, HEAD_DIM + pad, side * side * rows), bf16),
            pltpu.VMEM((HEAD_DIM + pad, side * side * rows), bf16),
            pltpu.VMEM((HEAD_DIM + pad, count), f32),
            pltpu.VMEM((1, count), f32),
            pltpu.VMEM((HEAD_DIM + pad, count), f32),
            pltpu.VMEM((1, count), f32),
            pltpu.VMEM((nz // 2, 2, side, rows, HEAD_DIM), bf16),
            pltpu.VMEM((side, 2, HEAD_DIM, group), bf16),
            pltpu.VMEM((side, 2, 8, group), f32),
            pltpu.VMEM((nz // 2, 2, side, rows, HEAD_DIM), bf16),
            pltpu.VMEM((2, side, HEAD_DIM, group), bf16),
            pltpu.VMEM((2, side, 8, group), f32),
            pltpu.VMEM((group, heads * HEAD_DIM), bf16),
            dma((3, nz)), dma((nz // 2,)), dma, dma, dma, dma, dma((nz,)), dma((nz,)),
            dma((nz // 2,)), dma, dma, dma,
            dma((3,)), dma((nz // 2, 2)), dma, dma, dma, dma, dma((nz,)), dma((nz,)),
            dma((nz // 2,)), dma, dma, dma((nz // 2,)), dma((nz // 2,)),
        ],
        compiler_params=pltpu.CompilerParams(
            collective_id=0, has_side_effects=True, vmem_limit_bytes=56 * 2**20
        ),
    )(queries, keys, values)
    velocity = moved.astype(jnp.float32)
    latent_next = latent + step_size * (1.5 * velocity - 0.5 * previous_velocity)
    return (velocity, latent_next)


def solution(mesh):
    in_specs = (
        P("cfg", ("blk", "uly"), None),
        P("cfg", ("blk", "uly"), None),
        P("cfg", ("blk", "uly"), None),
        P(("blk", "uly"), "cfg"),
        P(("blk", "uly"), "cfg"),
    )
    out_specs = (P(("blk", "uly"), "cfg"), P(("blk", "uly"), "cfg"))
    return jax.shard_map(
        on_device, mesh=mesh, in_specs=in_specs, out_specs=out_specs, check_vma=False
    )
```

```python
import functools
import math

import jax
import jax.numpy as jnp
from jax import lax
from jax.experimental import pallas as pl
from jax.experimental.pallas import tpu as pltpu
from jax.sharding import PartitionSpec as P

HEAD_DIM = 128

guidance_scale = 5.0
step_size = 0.25

EXP2_SCALE = math.log2(math.e) / math.sqrt(HEAD_DIM)
MESH = pl.DeviceIdType.MESH
MERGE_AT = 5
LATE = 1
CATCH_UP = 2
BEFORE = 4


def nt(left, right):
    return lax.dot_general(
        left, right, (((1,), (1,)), ((), ())), preferred_element_type=jnp.float32
    )


def kernel(
    nz, side, rows,
    q_ref, k_ref, v_ref, out_ref,
    line, kv, kv5, qm, q5, vt, vt5, acc, top, acc5, top5,
    o_send, p_send, l_send, o_got, p_got, l_got, merged,
    line_sem, q_sem, q5_sem, kv5_sem, q5f_sem, kv5f_sem, kv_sem, fwd_sem, o_sem, p_sem, l_sem, out_sem,
    line_sent, q_sent, q5_sent, kv5_sent, q5f_sent, kv5f_sent, kv_sent, fwd_sent,
    o_sent, p_sent, l_sent, out_sent, out5_sent,
):
    heads = side + 1
    half = nz // 2
    group = half * rows
    block = nz * rows
    queries = side * block
    tiles = (0, 1, 3, 2) if half == 4 else tuple(range(half))
    early, late = tiles[:half - LATE], tiles[half - LATE:]
    c = lax.axis_index("cfg")
    blk = lax.axis_index("blk")
    uly = lax.axis_index("uly")
    z = lax.div(blk, 2)
    x = lax.div(uly, side) * 2 + lax.rem(blk, 2)
    y = lax.rem(uly, side)
    a = x * (1 - c) + y * c
    b = y * (1 - c) + x * c

    def chip(x_, y_, z_, core):
        return (core, z_ * 2 + lax.rem(x_, 2), lax.div(x_, 2) * side + y_)

    def dev(a_, b_, z_, core=None):
        return chip(a_ * (1 - c) + b_ * c, b_ * (1 - c) + a_ * c, z_, c if core is None else core)

    def minus(value, steps, count):
        return lax.rem(value + count - steps, count)

    def plus(value, steps, count):
        return lax.rem(value + steps, count)

    def remote(src, dst, sent, got, device):
        return pltpu.make_async_remote_copy(
            src_ref=src, dst_ref=dst, send_sem=sent, recv_sem=got,
            device_id=device, device_id_type=MESH,
        )

    def await_bytes(ref, sem):
        pltpu.make_async_copy(ref, ref, sem).wait()

    barrier = pltpu.get_barrier_semaphore()

    def greet(device):
        pl.semaphore_signal(barrier, inc=1, device_id=device, device_id_type=MESH)

    def greet_layer(s, _):
        z_ = minus(z, s, nz)
        for r in range(side):
            greet(dev(minus(a, r, side), b, z_))
        greet(chip(x, y, z_, 1 - c))
        return 0

    for r in range(1, side):
        greet(dev(minus(a, r, side), b, z))
        greet(dev(a, minus(b, r, side), z))
        greet(chip(minus(x, r, side), y, z, 1 - c))
        greet(chip(x, minus(y, r, side), z, 1 - c))
    greet(chip(x, y, z, 1 - c))
    lax.fori_loop(1, nz, greet_layer, 0)
    pl.semaphore_wait(barrier, 4 * (side - 1) + 1 + (nz - 1) * (side + 1))

    others = pl.ds(1, side - 1)

    def cols(z_, head):
        return pl.ds(pl.multiple_of((z_ * heads + head) * HEAD_DIM, HEAD_DIM), HEAD_DIM)

    def order(i):
        odd = lax.rem(i, 2)
        later = lax.div(i, 2) + half * jnp.minimum(i, 1)
        return odd * lax.div(i + 1, 2) + (1 - odd) * later

    shared = (
        (q_ref, lambda s: q5.at[0, s], q5_sent, q5_sem),
        (k_ref, lambda s: kv5.at[0, 0, s], kv5_sent, kv5_sem),
        (v_ref, lambda s: kv5.at[1, 0, s], kv5_sent, kv5_sem),
    )

    def send_shared(i, _):
        s = order(i)
        z_ = minus(z, s, nz)
        for ref, place, sent, got in shared:
            remote(ref.at[0, :, cols(z_, side)], place(s), sent, got, dev(a, b, z_)).start()
        return 0

    def gather_line(part, s):
        ref = (q_ref, k_ref, v_ref)[part]
        z_ = minus(z, s, nz)
        first = isinstance(s, int) and s == 0
        if first:
            place = qm.at[0, 0] if part == 0 else kv.at[0, part - 1, 0]
            got = q_sem.at[0] if part == 0 else kv_sem.at[0]
        else:
            place = line.at[part, s]
            got = line_sem.at[part, s]
        pltpu.make_async_copy(ref.at[0, :, cols(z_, a)], place.at[0], got).start()
        for r in range(1, side):
            a_ = minus(a, r, side)
            remote(ref.at[0, :, cols(z_, a_)], place.at[r], line_sent.at[part], got,
                   dev(a_, b, z)).start()

    def gather_q(i, _):
        gather_line(0, order(i))
        return 0

    def gather_kv(i, _):
        gather_line(1, order(i))
        gather_line(2, order(i))
        return 0

    def send_q(t):
        for h in range(2):
            s = t + h * half
            if s:
                await_bytes(line.at[0, s], line_sem.at[0, s])
                remote(line.at[0, s], qm.at[t, h], q_sent.at[t, h], q_sem.at[t],
                       dev(a, b, minus(z, s, nz))).start()

    def sent_q(t):
        for h in range(2):
            if t or h:
                await_bytes(qm.at[t, h], q_sent.at[t, h])

    def send_kv(s):
        for part in range(2):
            await_bytes(line.at[part + 1, s], line_sem.at[part + 1, s])
            remote(line.at[part + 1, s], kv.at[s, part, 0], kv_sent.at[s], kv_sem.at[s],
                   dev(a, b, minus(z, s, nz))).start()

    def send_kv_layer(i, _):
        send_kv(order(i))
        return 0

    def forward(s):
        await_bytes(kv.at[s, :, 0], kv_sem.at[s])
        for r in (2, 1, 3)[:side - 1] if side > 2 else (1,):
            remote(kv.at[s, :, 0], kv.at[s, :, r], fwd_sent.at[s], fwd_sem.at[s],
                   dev(a, minus(b, r, side), z)).start()

    for ref, place, sent, got in shared:
        pltpu.make_async_copy(ref.at[0, :, cols(z, side)], place(0), got).start()
    lax.fori_loop(1, nz, send_shared, 0)
    gather_line(0, 0)
    lax.fori_loop(1, nz, gather_q, 0)
    gather_line(1, 0)
    gather_line(2, 0)
    lax.fori_loop(1, nz, gather_kv, 0)

    acc[...] = jnp.zeros_like(acc)
    top[...] = jnp.full_like(top, -1e30)
    acc5[...] = jnp.zeros_like(acc5)
    top5[...] = jnp.full_like(top5, -1e30)
    vt5[HEAD_DIM:, :] = jnp.ones((vt5.shape[0] - HEAD_DIM, vt5.shape[1]), vt5.dtype)
    for s in range(nz):
        vt[s, HEAD_DIM:, :] = jnp.ones((vt.shape[1] - HEAD_DIM, vt.shape[2]), vt.dtype)

    layers = pl.ds(1, nz - 1)
    await_bytes(q5.at[0, layers], q5_sent)
    await_bytes(kv5.at[:, 0, layers], kv5_sent)
    for t in early:
        send_q(t)

    await_bytes(q5.at[0], q5_sem)
    for r in range(1, side):
        remote(q5.at[0], q5.at[r], q5f_sent, q5f_sem, dev(minus(a, r, side), b, z)).start()
    await_bytes(kv5.at[:, 0], kv5_sem)
    for r in range(1, side):
        remote(kv5.at[:, 0], kv5.at[:, r], kv5f_sent, kv5f_sem, dev(a, minus(b, r, side), z)).start()

    lax.fori_loop(1, min(1 + BEFORE, nz), send_kv_layer, 0)
    for t in late:
        send_q(t)
    lax.fori_loop(min(1 + BEFORE, nz), nz, send_kv_layer, 0)

    def weigh(score, peak):
        return jnp.exp2((score - peak) * EXP2_SCALE).astype(jnp.bfloat16)

    def absorb(keys, values_t, parts, wide, rows_ref, total, largest, then=None):
        scores = [nt(keys, rows_ref[t].reshape(wide, HEAD_DIM)) for t in parts]
        for t, score in zip(parts, scores):
            at = pl.ds(t * wide, wide)
            old = largest[:, at]
            new = jnp.maximum(old, jnp.max(score, axis=0, keepdims=True))
            factor = jnp.exp2((old - new) * EXP2_SCALE)
            total[:, at] = total[:, at] * factor + jnp.dot(
                values_t[...], weigh(score, new), preferred_element_type=jnp.float32
            )
            largest[:, at] = new
            if then is not None:
                then(t, total[:, at])

    span = side * side * rows
    tile = 2 * side * rows
    chunks = nz // side
    split = side // chunks

    def absorb_shared(i, _):
        at = pl.ds(i * split, split)
        vt5[:HEAD_DIM, :] = kv5[1, at].reshape(span, HEAD_DIM).T
        absorb(kv5[0, at].reshape(span, HEAD_DIM), vt5, range(side), block, q5, acc5, top5)
        return 0

    await_bytes(q5.at[others], q5f_sem)
    await_bytes(kv5.at[:, others], kv5f_sem)
    forward(0)
    absorb_shared(0, 0)
    lax.fori_loop(1, chunks, absorb_shared, 0)

    def spread(r, moves):
        for h in range(2):
            def send():
                for src, dst, sent, got in moves(h):
                    remote(src, dst, sent, got, dev(plus(a, r, side), b, z, h)).start()

            def keep():
                for src, dst, sent, got in moves(h):
                    pltpu.make_async_copy(src, dst, got).start()

            if r:
                send()
            else:
                pl.when(c == h)(keep)
                pl.when(c != h)(send)

    for r in range(side):
        at = pl.ds(r * block, block)
        sums = acc5[HEAD_DIM:HEAD_DIM + 1, at]
        part = (acc5[:HEAD_DIM, at] / sums).astype(jnp.bfloat16)
        log_sum = jnp.broadcast_to(top5[:, at] * EXP2_SCALE + jnp.log2(sums), (8, block))
        for h in range(2):
            p_send[r, h] = part[:, h * group:(h + 1) * group]
            l_send[r, h] = log_sum[:, h * group:(h + 1) * group]
        spread(r, lambda h: (
            (p_send.at[r, h], p_got.at[c, r], p_sent, p_sem),
            (l_send.at[r, h], l_got.at[c, r], l_sent, l_sem),
        ))

    def guided(conditional, unconditional):
        return unconditional + guidance_scale * (conditional - unconditional)

    width = heads * HEAD_DIM
    target = lax.div(z, half)
    at_home = (c == 0) & (target == 0)

    def deliver(first, count, sent, *slots):
        start = pl.multiple_of(lax.rem(z, half) * width + first * HEAD_DIM, HEAD_DIM)
        place = out_ref.at[:, pl.ds(start, count * HEAD_DIM)]
        for j in slots or range(half):
            src = merged.at[pl.ds(j * rows, rows), pl.ds(first * HEAD_DIM, count * HEAD_DIM)]

            def send():
                remote(src, place, sent.at[j], out_sem,
                       chip(x, y, plus(z, c * half + j, nz), target)).start()

            def keep():
                pltpu.make_async_copy(src, place, out_sem).start()

            if j:
                send()
            else:
                pl.when(at_home)(keep)
                pl.when(jnp.logical_not(at_home))(send)

    def delivered(first, count, sent):
        for j in range(half):
            src = merged.at[pl.ds(j * rows, rows), pl.ds(first * HEAD_DIM, count * HEAD_DIM)]
            if j:
                await_bytes(src, sent.at[j])
            else:
                pl.when(jnp.logical_not(at_home))(lambda: await_bytes(src, sent.at[0]))

    def merge_shared():
        await_bytes(p_got, p_sem)
        await_bytes(l_got, l_sem)
        joined = []
        for branch in range(2):
            log_sums = [l_got[branch, r][:1] for r in range(side)]
            largest = functools.reduce(jnp.maximum, log_sums)
            shares = [jnp.exp2(value - largest) for value in log_sums]
            total = sum(shares)
            joined.append(
                sum(p_got[branch, r].astype(jnp.float32) * (shares[r] / total) for r in range(side))
            )
        merged[:, side * HEAD_DIM:] = guided(*joined).T.astype(jnp.bfloat16)
        deliver(side, 1, out5_sent)

    for t in early:
        await_bytes(qm.at[t], q_sem.at[t])

    def step(i, then):
        s = order(i)
        await_bytes(kv.at[s, :, others], fwd_sem.at[s])
        vt[s, :HEAD_DIM, :] = kv[s, 1].reshape(span, HEAD_DIM).T
        absorb(kv[s, 0].reshape(span, HEAD_DIM), vt.at[s], early, tile, qm, acc, top, then)

    def prepared_step(i, _):
        forward(order(i + 1))
        pl.when(i == MERGE_AT)(merge_shared)
        step(i, None)

        @pl.when(i == nz - CATCH_UP)
        def _():
            for t in late:
                await_bytes(qm.at[t], q_sem.at[t])
                attend(t, 0, half, False)

        return 0

    def finish(t, total):
        own = (total[:HEAD_DIM] / total[HEAD_DIM:HEAD_DIM + 1]).T
        o_send[t] = own.astype(jnp.bfloat16).reshape(2, side, rows, HEAD_DIM)
        for r in range(side):
            spread(r, lambda h: ((o_send.at[t, h, r], o_got.at[t, c, a], o_sent.at[t], o_sem.at[t]),))

    def merge(t):
        await_bytes(o_got.at[t], o_sem.at[t])
        for head in range(side):
            merged[t * rows:(t + 1) * rows, head * HEAD_DIM:(head + 1) * HEAD_DIM] = guided(
                o_got[t, 0, head].astype(jnp.float32), o_got[t, 1, head].astype(jnp.float32)
            ).astype(jnp.bfloat16)
        deliver(0, side, out_sent, t)


    sequence = [0] + [(i + 1) // 2 if i % 2 else i // 2 + half for i in range(1, nz)]

    def attend(t, first, stop, last):
        at = pl.ds(t * tile, tile)
        own = qm[t].reshape(tile, HEAD_DIM)

        def score(s):
            return nt(kv[s, 0].reshape(span, HEAD_DIM), own)

        pairs = [sequence[i:i + 2] for i in range(first, stop, 2)]
        ready = [score(s) for s in pairs[0]]
        peak, total = top[:, at], acc[:, at]
        for index, pair in enumerate(pairs):
            following = [score(s) for s in pairs[index + 1]] if index + 1 < len(pairs) else None
            new = peak
            for value in ready:
                new = jnp.maximum(new, jnp.max(value, axis=0, keepdims=True))
            total = total * jnp.exp2((peak - new) * EXP2_SCALE)
            for s, value in zip(pair, ready):
                total = total + jnp.dot(vt[s], weigh(value, new), preferred_element_type=jnp.float32)
            peak, ready = new, following
        if last:
            finish(t, total)
        else:
            acc[:, at], top[:, at] = total, peak

    lax.fori_loop(0, nz - 1, prepared_step, 0)
    step(jnp.int32(nz - 1), finish)

    waiting = list(early)
    for t in late:
        attend(t, half, nz, True)
        for done in waiting:
            merge(done)
        waiting = [t]
    for done in waiting:
        merge(done)

    for part in range(3):
        await_bytes(line.at[part, :, others], line_sent.at[part])

    def sent_layer(s, _):
        await_bytes(kv.at[s, :, 0], kv_sent.at[s])
        return 0

    lax.fori_loop(1, nz, sent_layer, 0)

    def sent_forward(s, _):
        await_bytes(kv.at[s, :, others], fwd_sent.at[s])
        return 0

    lax.fori_loop(0, nz, sent_forward, 0)
    await_bytes(q5.at[others], q5f_sent)
    await_bytes(kv5.at[:, others], kv5f_sent)
    for buffer, sem in ((p_send, p_sent), (l_send, l_sent)):
        await_bytes(buffer.at[others], sem)
        await_bytes(buffer.at[0, 0], sem)
    for t in range(half):
        await_bytes(o_send.at[t, :, others], o_sent.at[t])
        await_bytes(o_send.at[t, 0, 0], o_sent.at[t])
    for t in tiles:
        sent_q(t)
    delivered(side, 1, out5_sent)
    delivered(0, side, out_sent)
    await_bytes(out_ref, out_sem)


def on_device(queries, keys, values, latent, previous_velocity):
    nz = lax.axis_size("blk") // 2
    side = math.isqrt(lax.axis_size("uly") * 2)
    rows = queries.shape[1]
    columns = queries.shape[2] // 2
    heads = side + 1
    group = nz // 2 * rows
    count = side * nz * rows
    pad = 16
    dma = pltpu.SemaphoreType.DMA
    bf16, f32 = jnp.bfloat16, jnp.float32
    moved = pl.pallas_call(
        functools.partial(kernel, nz, side, rows),
        out_shape=jax.ShapeDtypeStruct((rows, columns), bf16),
        in_specs=[pl.BlockSpec(memory_space=pl.ANY)] * 3,
        out_specs=pl.BlockSpec(memory_space=pl.ANY),
        scratch_shapes=[
            pltpu.VMEM((3, nz, side, rows, HEAD_DIM), bf16),
            pltpu.VMEM((nz, 2, side, side, rows, HEAD_DIM), bf16),
            pltpu.VMEM((2, side, nz, rows, HEAD_DIM), bf16),
            pltpu.VMEM((nz // 2, 2, side, rows, HEAD_DIM), bf16),
            pltpu.VMEM((side, nz, rows, HEAD_DIM), bf16),
            pltpu.VMEM((nz, HEAD_DIM + pad, side * side * rows), bf16),
            pltpu.VMEM((HEAD_DIM + pad, side * side * rows), bf16),
            pltpu.VMEM((HEAD_DIM + pad, count), f32),
            pltpu.VMEM((1, count), f32),
            pltpu.VMEM((HEAD_DIM + pad, count), f32),
            pltpu.VMEM((1, count), f32),
            pltpu.VMEM((nz // 2, 2, side, rows, HEAD_DIM), bf16),
            pltpu.VMEM((side, 2, HEAD_DIM, group), bf16),
            pltpu.VMEM((side, 2, 8, group), f32),
            pltpu.VMEM((nz // 2, 2, side, rows, HEAD_DIM), bf16),
            pltpu.VMEM((2, side, HEAD_DIM, group), bf16),
            pltpu.VMEM((2, side, 8, group), f32),
            pltpu.VMEM((group, heads * HEAD_DIM), bf16),
            dma((3, nz)), dma((nz // 2,)), dma, dma, dma, dma, dma((nz,)), dma((nz,)),
            dma((nz // 2,)), dma, dma, dma,
            dma((3,)), dma((nz // 2, 2)), dma, dma, dma, dma, dma((nz,)), dma((nz,)),
            dma((nz // 2,)), dma, dma, dma((nz // 2,)), dma((nz // 2,)),
        ],
        compiler_params=pltpu.CompilerParams(
            collective_id=0, has_side_effects=True, vmem_limit_bytes=56 * 2**20
        ),
    )(queries, keys, values)
    velocity = moved.astype(jnp.float32)
    latent_next = latent + step_size * (1.5 * velocity - 0.5 * previous_velocity)
    return (velocity, latent_next)


def solution(mesh):
    in_specs = (
        P("cfg", ("blk", "uly"), None),
        P("cfg", ("blk", "uly"), None),
        P("cfg", ("blk", "uly"), None),
        P(("blk", "uly"), "cfg"),
        P(("blk", "uly"), "cfg"),
    )
    out_specs = (P(("blk", "uly"), "cfg"), P(("blk", "uly"), "cfg"))
    return jax.shard_map(
        on_device, mesh=mesh, in_specs=in_specs, out_specs=out_specs, check_vma=False
    )
```
